256 devices in a mesh: leaf: 2 (over core), row: 16 (over y, x), col: 8 (over z).
Axes of the slice: x: 4, y: 4, z: 8, core: 2. Of those that a mesh axis runs over, the one named last changes fastest.
Arguments:
- ancestor_inverse: bfloat16 [16384, 16384], P(('leaf', 'col'), 'row'), may hold values from -6 to 6
- panels: bfloat16 [16384, 4096], P('row', ('leaf', 'col')), may hold values from -0.046875 to 0.046875
- pattern: int32 [64, 16], replicated, may hold values from 0 to 1
- diag_inverse: float32 [16, 256, 256], P('row'), may hold values from -6 to 6
Outputs:
- covariance: float32 [16384, 4096], P(('leaf', 'col'), 'row')
- diag_cov: float32 [16, 256, 256], P('row')
The draws below stay inside these ranges and needn't reach their ends.
All inputs are finite; a program needn't handle non-finite values.
Results may differ from the reference program's by a relative error of at most 0.0003.
Values may be sent and summed in bfloat16 or wider, within the bound.
A program may use at most 128 MiB of HBM per device.

```python
import jax
import jax.numpy as jnp
from jax import lax

BLOCK = 256
NA = 64
SN = 16
N_ROW = 16


def draw_pattern(key, part):
    key = jax.random.fold_in(key, 11)
    ranks = jax.random.randint(key, (NA, SN), 0, NA)
    levels = jnp.arange(NA, dtype=jnp.int32)[:, None] + NA // 4
    return (ranks <= levels).astype(jnp.int32)


def shard_levels(stream_key, extent, cuts, low, largest):
    factor_of = 1.0
    for position, shards_of in cuts:
        draws = jax.random.uniform(jax.random.fold_in(jax.random.fold_in(stream_key, 6), position), (shards_of,), jnp.float32, low / len(cuts), largest / len(cuts))
        factor_of = factor_of * jnp.repeat(jnp.exp(draws), extent[position] // shards_of).reshape((-1,) + (1,) * (len(extent) - 1 - position))
    return factor_of


def gaussian(rng, shape, spread, bound, pieces=(), kind=jnp.bfloat16):
    drawn = spread * jax.random.normal(rng, shape, jnp.float32)
    if pieces:
        drawn = drawn * shard_levels(rng, shape, pieces, -0.22, 0.18)
    return jnp.clip(drawn, -bound, bound).astype(kind)


def setup_inputs(seed: int = 0) -> dict:
    arg_keys = jax.random.split(jax.random.key(seed), 5)
    return {
        "ancestor_inverse": gaussian(arg_keys[0], (NA * BLOCK, NA * BLOCK), 1.0, 6.0, ((0, 16), (1, 16))),
        "panels": gaussian(arg_keys[1], (NA * BLOCK, SN * BLOCK), (NA * BLOCK) ** -0.5, 0.046875, ((0, 16), (1, 16))),
        "pattern": draw_pattern(jax.random.fold_in(arg_keys[4], 71), 0),
        "diag_inverse": gaussian(arg_keys[3], (SN, BLOCK, BLOCK), 1.0, 6.0, ((0, 16),), jnp.float32),
    }


def apply_pattern(matrix, pattern, dtype):
    shaped = matrix.reshape(NA, BLOCK, SN, BLOCK)
    return (shaped * pattern[:, None, :, None].astype(dtype)).reshape(NA * BLOCK, SN * BLOCK)


def reference(ancestor_inverse, panels, pattern, diag_inverse):
    masked = apply_pattern(panels, pattern, jnp.bfloat16)
    stripe_width = NA * BLOCK // N_ROW
    product = jnp.zeros((NA * BLOCK, SN * BLOCK), jnp.float32)
    for stripe in range(N_ROW):
        partial_value = jnp.dot(ancestor_inverse[:, stripe * stripe_width:(stripe + 1) * stripe_width],
                          masked[stripe * stripe_width:(stripe + 1) * stripe_width],
                          preferred_element_type=jnp.float32)
        product = product + partial_value
    covariance = -apply_pattern(product, pattern, jnp.float32)
    columns = masked.astype(jnp.float32).reshape(NA * BLOCK, SN, BLOCK)
    results = product.reshape(NA * BLOCK, SN, BLOCK)
    terms = jnp.einsum("nsa,nsb->sab", columns, results, precision=lax.Precision.HIGHEST)
    diag_cov = diag_inverse + terms
    return covariance, diag_cov
```

```python
import jax
import jax.numpy as jnp
from jax import lax
from jax.experimental import pallas as pl
from jax.experimental.pallas import tpu as pltpu
from jax.sharding import PartitionSpec as P

MESH = pl.DeviceIdType.MESH
SIDE = 4
LANES = 128
OFFSETS = (2, 1, 3, 0)


def kernel(
    pattern, a_ref, panel, dinv, cov, diag,
    mbuf, match, pbuf, r1, r2, r3, r4, term, dpart, dsum,
    zs, zr, ls, lr, s1, q1, s2, q2, s3, q3, s4, q4, ts, tr, ps, pr, bs, br,
):
    nz = lax.axis_size("col")
    leaf = lax.axis_index("leaf")
    row = lax.axis_index("row")
    z = lax.axis_index("col")
    y = row // SIDE
    x = lax.rem(row, SIDE)
    groups = 2 * nz
    group = leaf * nz + z
    depth = panel.shape[0]
    block = dinv.shape[1]
    blocks = depth // block
    half = depth // 2
    quarter = depth // 4
    chunks = block // LANES
    piece = block // groups

    def peer(j):
        p = lax.rem(group + j, groups)
        return (p // nz, row, lax.rem(p, nz))

    def z_dev(step):
        return (leaf, row, lax.rem(z + step + nz, nz))

    def x_dev(step):
        return (leaf, y * SIDE + lax.rem(x + step + SIDE, SIDE), z)

    def y_dev(step):
        return (leaf, lax.rem(y + step + SIDE, SIDE) * SIDE + x, z)

    other = (1 - leaf, row, z)
    swapped = (row // nz, group, lax.rem(row, nz))
    moves = row != group

    def remote(src, dst, send, recv, dev):
        return pltpu.make_async_remote_copy(
            src_ref=src, dst_ref=dst, send_sem=send, recv_sem=recv,
            device_id=dev, device_id_type=MESH,
        )

    barrier = pltpu.get_barrier_semaphore()

    @pl.loop(1, groups)
    def _(j):
        pl.semaphore_signal(barrier, inc=1, device_id=peer(j), device_id_type=MESH)

    for dev in (x_dev(1), x_dev(-1), y_dev(1), y_dev(-1)):
        pl.semaphore_signal(barrier, inc=1, device_id=dev, device_id_type=MESH)

    @pl.when(moves)
    def _():
        pl.semaphore_signal(barrier, inc=1, device_id=swapped, device_id_type=MESH)

    for c in range(chunks):
        for i in range(blocks):
            keep = pattern[row * blocks + i, group].astype(jnp.float32)
            rows = pl.ds(i * block, block)
            values = panel[rows, pl.ds(c * LANES, LANES)].astype(jnp.float32) * keep
            mbuf[c, group, rows, :] = values.astype(jnp.bfloat16)

    pl.semaphore_wait(barrier, groups - 1 + 4 + moves.astype(jnp.int32))

    turns = nz // 2
    pieces = 2 * turns - 1

    def z_rows(way, j):
        h = j % 2 if way == 0 else 1 - j % 2
        return pl.ds(h * half, half)

    def z_copy(c, way, j, lag):
        step = -1 if way == 0 else 1
        s = leaf * nz + lax.rem(z + step * (j // 2 + lag) + 2 * nz, nz)
        view = mbuf.at[c, s, z_rows(way, j), :]
        return remote(view, view, zs.at[c, way, j], zr.at[c, way, j], z_dev(-step))

    def leaf_copy(c, way, j, lf):
        step = -1 if way == 0 else 1
        s = lf * nz + lax.rem(z + step * (j // 2 + 1) + 2 * nz, nz)
        view = mbuf.at[c, s, z_rows(way, j), :]
        n = way * pieces + j
        return remote(view, view, ls.at[c, n], lr.at[c, n], other)

    def leaf_own(c, lf):
        view = mbuf.at[c, lf * nz + z]
        return remote(view, view, ls.at[c, 2 * pieces], lr.at[c, 2 * pieces], other)

    def gather_begin(c):
        for j in range(2):
            for way in range(2):
                z_copy(c, way, j, 0).start()
        leaf_own(c, leaf).start()

    def gather_step(c, d):
        for j in range(2 * d, min(2 * d + 2, pieces)):
            for way in range(2):
                z_copy(c, way, j, 1).wait_recv()
                if j + 2 < pieces:
                    z_copy(c, way, j + 2, 0).start()
                leaf_copy(c, way, j, leaf).start()

    def multiply(c, sa, sb):
        @pl.loop(0, a_ref.shape[0] // 256)
        def _(t):
            rows = pl.ds(pl.multiple_of(t * 256, 256), 256)
            right = jnp.concatenate([mbuf[c, sa], mbuf[c, sb]], axis=1)
            out = jnp.dot(a_ref[rows, :], right, preferred_element_type=jnp.float32)
            pbuf[c, sa, rows, :] = out[:, :LANES]
            pbuf[c, sb, rows, :] = out[:, LANES:]

    def products(c, d):
        if d == 0:
            leaf_own(c, 1 - leaf).wait_recv()
            multiply(c, leaf * nz + z, (1 - leaf) * nz + z)
            return
        for j in range(2 * d - 2, min(2 * d, pieces)):
            for way in range(2):
                leaf_copy(c, way, j, 1 - leaf).wait_recv()
        up = lax.rem(z + d, nz)
        down = lax.rem(z + nz - d, nz)
        if d == turns:
            multiply(c, leaf * nz + up, (1 - leaf) * nz + up)
        else:
            multiply(c, leaf * nz + up, leaf * nz + down)
            multiply(c, (1 - leaf) * nz + up, (1 - leaf) * nz + down)

    def first(f):
        return (x, y)[f]

    def second(f):
        return (y, x)[f]

    def dev_first(f, step):
        return (x_dev, y_dev)[f](step)

    def dev_second(f, step):
        return (y_dev, x_dev)[f](step)

    def part(c, f, df, k, lo, n):
        a = lax.rem(first(f) + df, SIDE)
        b = lax.rem(second(f) + OFFSETS[k], SIDE)
        s = b * SIDE + a if f == 0 else a * SIDE + b
        return pbuf.at[c, s, pl.ds(f * half + lo, n), :]

    def far(c, f, way, k):
        return remote(
            part(c, f, 2, k, way * quarter, quarter), r1.at[c, f, way, k],
            s1.at[c, f, way, k], q1.at[c, f, way, k], dev_first(f, 1 - 2 * way),
        )

    def near(c, f, way, k):
        return remote(
            part(c, f, 1 + 2 * way, k, 0, half), r2.at[c, f, way, k],
            s2.at[c, f, way, k], q2.at[c, f, way, k], dev_first(f, 1 - 2 * way),
        )

    def far_second(c, f, way):
        return remote(
            part(c, f, 0, 0, way * quarter, quarter), r3.at[c, f, way],
            s3.at[c, f, way], q3.at[c, f, way], dev_second(f, 1 - 2 * way),
        )

    def near_second(c, f, way):
        return remote(
            part(c, f, 0, 1 + way, 0, half), r4.at[c, f, way],
            s4.at[c, f, way], q4.at[c, f, way], dev_second(f, 1 - 2 * way),
        )

    def send_far(c, k):
        for f in range(2):
            for way in range(2):
                far(c, f, way, k).start()

    def send_near(c, k):
        for f in range(2):
            for way in range(2):
                far(c, f, way, k).wait_recv()
                own = part(c, f, 1 + 2 * way, k, way * quarter, quarter)
                own[...] = own[...] + r1[c, f, way, k]
                near(c, f, way, k).start()

    def turn(c, k):
        for f in range(2):
            for way in range(2):
                near(c, f, way, k).wait_recv()
            own = part(c, f, 0, k, 0, half)
            own[...] = own[...] + (r2[c, f, 0, k] + r2[c, f, 1, k])
            if k == 0:
                far_second(c, f, 0).start()
                far_second(c, f, 1).start()
            elif k < 3:
                way = k - 1
                far_second(c, f, way).wait_recv()
                own = part(c, f, 0, k, way * quarter, quarter)
                own[...] = own[...] + r3[c, f, way]
                near_second(c, f, way).start()

    def swap(c):
        return remote(mbuf.at[c, group], match.at[c], ts.at[c], tr.at[c], swapped)

    def finish(c):
        for f in range(2):
            for way in range(2):
                near_second(c, f, way).wait_recv()
            own = part(c, f, 0, 3, 0, half)
            own[...] = own[...] + (r4[c, f, 0] + r4[c, f, 1])
        product = pbuf.at[c, row]

        if c == 0:
            @pl.when(moves)
            def _():
                for e in range(chunks):
                    swap(e).wait_recv()

        value = product[...]
        total = None
        rest = value
        columns = jnp.concatenate([match[e] for e in range(chunks)], axis=1)
        for _ in range(3):
            top = rest.astype(jnp.bfloat16)
            rest = rest - top.astype(jnp.float32)
            add = lax.dot_general(
                columns, top, (((0,), (0,)), ((), ())), preferred_element_type=jnp.float32
            )
            total = add if total is None else total + add
        term[c] = total

        @pl.loop(1, groups)
        def _(j):
            give(c, j).start()

        for i in range(blocks):
            keep = pattern[group * blocks + i, row].astype(jnp.float32)
            rows = pl.ds(i * block, block)
            cov[rows, pl.ds(c * LANES, LANES)] = -(product[rows, :] * keep)

    def give(c, j):
        to = lax.rem(group + j, groups)
        rows = pl.ds(pl.multiple_of(to * piece, piece), piece)
        return remote(term.at[c, rows, :], dpart.at[c, j], ps.at[c, j], pr.at[c, j], peer(j))

    def mine(owner):
        return pl.ds(pl.multiple_of(owner * piece, piece), piece)

    def spread(c, j, owner):
        view = dsum.at[c, mine(owner), :]
        return remote(view, view, bs.at[c, j], br.at[c, j], peer(j))

    def settle(c):
        @pl.loop(1, groups)
        def _(j):
            give(c, j).wait_recv()

        dsum[c, mine(group), :] = (
            dinv[0, mine(group), pl.ds(c * LANES, LANES)]
            + (term[c, mine(group), :] + jnp.sum(dpart[c, pl.ds(1, groups - 1)], axis=0))
        )

        @pl.loop(1, groups)
        def _(j):
            spread(c, j, group).start()

    def collect(c):
        @pl.loop(1, groups)
        def _(j):
            spread(c, j, lax.rem(group - j + groups, groups)).wait_recv()

        diag[0, :, pl.ds(c * LANES, LANES)] = dsum[c]

    gather_begin(0)
    products(0, 0)
    for d in range(turns):
        gather_step(0, d)
        if d == turns - 2:
            gather_begin(1)
            @pl.when(moves)
            def _():
                for c in range(chunks):
                    swap(c).start()

            @pl.when(jnp.logical_not(moves))
            def _():
                for c in range(chunks):
                    match[c] = mbuf[c, group]
        if d > 0:
            products(0, d)
    products(0, turns)
    for k in range(4):
        send_far(0, k)
    products(1, 0)
    for k in range(4):
        gather_step(1, k)
        send_near(0, k)
        products(1, k + 1)
    for k in range(4):
        send_far(1, k)
    for k in range(4):
        turn(0, k)
        send_near(1, k)
    finish(0)
    for k in range(4):
        turn(1, k)
    settle(0)
    finish(1)
    collect(0)
    settle(1)
    collect(1)

    for c in range(chunks):
        leaf_own(c, leaf).wait_send()
        for way in range(2):
            for j in range(pieces):
                z_copy(c, way, j, 0).wait_send()
                leaf_copy(c, way, j, leaf).wait_send()
            for f in range(2):
                for k in range(4):
                    far(c, f, way, k).wait_send()
                    near(c, f, way, k).wait_send()
                far_second(c, f, way).wait_send()
                near_second(c, f, way).wait_send()

        @pl.loop(1, groups)
        def _(j):
            give(c, j).wait_send()
            spread(c, j, group).wait_send()

        @pl.when(moves)
        def _():
            swap(c).wait_send()


def local(ancestor_inverse, panels, pattern, diag_inverse):
    depth, width = panels.shape
    rows_out = ancestor_inverse.shape[0]
    block = diag_inverse.shape[1]
    nz = lax.axis_size("col")
    groups = 2 * nz
    supers = pattern.shape[1]
    chunks = block // LANES
    half, quarter = depth // 2, depth // 4
    f32, bf16 = jnp.float32, jnp.bfloat16
    pieces = 2 * (nz // 2) - 1
    dma = pltpu.SemaphoreType.DMA
    vmem = pl.BlockSpec(memory_space=pltpu.VMEM)
    sems = [
        (chunks, 2, pieces), (chunks, 2 * pieces + 1),
        (chunks, 2, 2, 4), (chunks, 2, 2, 4), (chunks, 2, 2), (chunks, 2, 2),
        (chunks,), (chunks, groups), (chunks, groups),
    ]
    return tuple(pl.pallas_call(
        kernel,
        out_shape=(
            jax.ShapeDtypeStruct((rows_out, width), f32),
            jax.ShapeDtypeStruct(diag_inverse.shape, f32),
        ),
        in_specs=[pl.BlockSpec(memory_space=pltpu.SMEM), vmem, vmem, vmem],
        out_specs=(vmem, vmem),
        scratch_shapes=[
            pltpu.VMEM((chunks, supers, depth, LANES), bf16),
            pltpu.VMEM((chunks, depth, LANES), bf16),
            pltpu.VMEM((chunks, supers, rows_out, LANES), f32),
            pltpu.VMEM((chunks, 2, 2, 4, quarter, LANES), f32),
            pltpu.VMEM((chunks, 2, 2, 4, half, LANES), f32),
            pltpu.VMEM((chunks, 2, 2, quarter, LANES), f32),
            pltpu.VMEM((chunks, 2, 2, half, LANES), f32),
            pltpu.VMEM((chunks, block, LANES), f32),
            pltpu.VMEM((chunks, groups, block // groups, LANES), f32),
            pltpu.VMEM((chunks, block, LANES), f32),
        ] + [dma(s) for s in sems for _ in range(2)],
        compiler_params=pltpu.CompilerParams(
            collective_id=0, has_side_effects=True, vmem_limit_bytes=58 * 2**20
        ),
        cost_estimate=pl.CostEstimate(
            flops=2 * rows_out * depth * supers * block, bytes_accessed=8 * 2**20, transcendentals=0
        ),
    )(pattern, ancestor_inverse, panels, diag_inverse))


def solution(mesh):
    placed = (P(("leaf", "col"), "row"), P("row", ("leaf", "col")), P(), P("row", None, None))
    return jax.shard_map(
        local,
        mesh=mesh,
        in_specs=placed,
        out_specs=(P(("leaf", "col"), "row"), P("row", None, None)),
        check_vma=False,
    )
```

```python
import jax
import jax.numpy as jnp
from jax import lax
from jax.experimental import pallas as pl
from jax.experimental.pallas import tpu as pltpu
from jax.sharding import PartitionSpec as P

MESH = pl.DeviceIdType.MESH
SIDE = 4
LANES = 128
OFFSETS = (2, 1, 3, 0)


def kernel(
    pattern, a_ref, panel, dinv, cov, diag,
    mbuf, match, relay, pbuf, r1, r2, r3, r4, term, dpart, dsum,
    zs, zr, ls, lr, s1, q1, s2, q2, s3, q3, s4, q4, ts, tr, ps, pr, bs, br,
):
    nz = lax.axis_size("col")
    leaf = lax.axis_index("leaf")
    row = lax.axis_index("row")
    z = lax.axis_index("col")
    y = row // SIDE
    x = lax.rem(row, SIDE)
    groups = 2 * nz
    group = leaf * nz + z
    depth = panel.shape[0]
    block = dinv.shape[1]
    blocks = depth // block
    half = depth // 2
    quarter = depth // 4
    chunks = block // LANES
    piece = block // groups

    def peer(j):
        p = lax.rem(group + j, groups)
        return (p // nz, row, lax.rem(p, nz))

    def z_dev(step):
        return (leaf, row, lax.rem(z + step + nz, nz))

    def x_dev(step):
        return (leaf, y * SIDE + lax.rem(x + step + SIDE, SIDE), z)

    def y_dev(step):
        return (leaf, lax.rem(y + step + SIDE, SIDE) * SIDE + x, z)

    other = (1 - leaf, row, z)
    held = leaf * nz + lax.rem(z + 2 * leaf + row, nz)
    taker = (row // nz, held, z)
    turned = lax.rem(row - z - 2 * (row // nz) + 2 * nz, nz)
    giver = (row // nz, leaf * nz + turned, z)
    moves = jnp.logical_or(row // nz != leaf, held != row)
    onward = (leaf, row, turned)
    goes_on = turned != z

    def remote(src, dst, send, recv, dev):
        return pltpu.make_async_remote_copy(
            src_ref=src, dst_ref=dst, send_sem=send, recv_sem=recv,
            device_id=dev, device_id_type=MESH,
        )

    barrier = pltpu.get_barrier_semaphore()

    @pl.loop(1, groups)
    def _(j):
        pl.semaphore_signal(barrier, inc=1, device_id=peer(j), device_id_type=MESH)

    for dev in (x_dev(1), x_dev(-1), y_dev(1), y_dev(-1)):
        pl.semaphore_signal(barrier, inc=1, device_id=dev, device_id_type=MESH)

    @pl.when(moves)
    def _():
        pl.semaphore_signal(barrier, inc=1, device_id=giver, device_id_type=MESH)

    for c in range(chunks):
        for i in range(blocks):
            keep = pattern[group, row * blocks + i].astype(jnp.float32)
            rows = pl.ds(i * block, block)
            values = panel[rows, pl.ds(c * LANES, LANES)].astype(jnp.float32) * keep
            mbuf[c, group, rows, :] = values.astype(jnp.bfloat16)

    pl.semaphore_wait(barrier, groups - 1 + 4 + moves.astype(jnp.int32))

    turns = nz // 2
    pieces = 2 * turns - 1

    def z_rows(way, j):
        h = j % 2 if way == 0 else 1 - j % 2
        return pl.ds(h * half, half)

    def z_copy(c, way, j, lag):
        step = -1 if way == 0 else 1
        s = leaf * nz + lax.rem(z + step * (j // 2 + lag) + 2 * nz, nz)
        view = mbuf.at[c, s, z_rows(way, j), :]
        return remote(view, view, zs.at[c, way, j], zr.at[c, way, j], z_dev(-step))

    def leaf_copy(c, way, j, lf):
        step = -1 if way == 0 else 1
        s = lf * nz + lax.rem(z + step * (j // 2 + 1) + 2 * nz, nz)
        view = mbuf.at[c, s, z_rows(way, j), :]
        n = way * pieces + j
        return remote(view, view, ls.at[c, n], lr.at[c, n], other)

    def leaf_own(c, lf):
        view = mbuf.at[c, lf * nz + z]
        return remote(view, view, ls.at[c, 2 * pieces], lr.at[c, 2 * pieces], other)

    def gather_begin(c):
        for j in range(2):
            for way in range(2):
                z_copy(c, way, j, 0).start()
        leaf_own(c, leaf).start()

    def gather_step(c, d):
        for j in range(2 * d, min(2 * d + 2, pieces)):
            for way in range(2):
                z_copy(c, way, j, 1).wait_recv()
                if j + 2 < pieces:
                    z_copy(c, way, j + 2, 0).start()
                leaf_copy(c, way, j, leaf).start()

    def multiply(c, sa, sb):
        @pl.loop(0, a_ref.shape[0] // 256)
        def _(t):
            rows = pl.ds(pl.multiple_of(t * 256, 256), 256)
            right = jnp.concatenate([mbuf[c, sa], mbuf[c, sb]], axis=1)
            out = jnp.dot(a_ref[rows, :], right, preferred_element_type=jnp.float32)
            pbuf[c, sa, rows, :] = out[:, :LANES]
            pbuf[c, sb, rows, :] = out[:, LANES:]

    def products(c, d):
        if d == 0:
            leaf_own(c, 1 - leaf).wait_recv()
            multiply(c, leaf * nz + z, (1 - leaf) * nz + z)
            return
        for j in range(2 * d - 2, min(2 * d, pieces)):
            for way in range(2):
                leaf_copy(c, way, j, 1 - leaf).wait_recv()
        up = lax.rem(z + d, nz)
        down = lax.rem(z + nz - d, nz)
        if d == turns:
            multiply(c, leaf * nz + up, (1 - leaf) * nz + up)
        else:
            multiply(c, leaf * nz + up, leaf * nz + down)
            multiply(c, (1 - leaf) * nz + up, (1 - leaf) * nz + down)

    def first(f):
        return (x, y)[f]

    def second(f):
        return (y, x)[f]

    def dev_first(f, step):
        return (x_dev, y_dev)[f](step)

    def dev_second(f, step):
        return (y_dev, x_dev)[f](step)

    def part(c, f, df, k, lo, n):
        a = lax.rem(first(f) + df, SIDE)
        b = lax.rem(second(f) + OFFSETS[k], SIDE)
        s = b * SIDE + a if f == 0 else a * SIDE + b
        return pbuf.at[c, s, pl.ds(f * half + lo, n), :]

    def far(c, f, way, k):
        return remote(
            part(c, f, 2, k, way * quarter, quarter), r1.at[c, f, way, k],
            s1.at[c, f, way, k], q1.at[c, f, way, k], dev_first(f, 1 - 2 * way),
        )

    def near(c, f, way, k):
        return remote(
            part(c, f, 1 + 2 * way, k, 0, half), r2.at[c, f, way, k],
            s2.at[c, f, way, k], q2.at[c, f, way, k], dev_first(f, 1 - 2 * way),
        )

    def far_second(c, f, way):
        return remote(
            part(c, f, 0, 0, way * quarter, quarter), r3.at[c, f, way],
            s3.at[c, f, way], q3.at[c, f, way], dev_second(f, 1 - 2 * way),
        )

    def near_second(c, f, way):
        return remote(
            part(c, f, 0, 1 + way, 0, half), r4.at[c, f, way],
            s4.at[c, f, way], q4.at[c, f, way], dev_second(f, 1 - 2 * way),
        )

    def send_far(c, k):
        for f in range(2):
            for way in range(2):
                far(c, f, way, k).start()

    def send_near(c, k):
        for f in range(2):
            for way in range(2):
                far(c, f, way, k).wait_recv()
                own = part(c, f, 1 + 2 * way, k, way * quarter, quarter)
                own[...] = own[...] + r1[c, f, way, k]
                near(c, f, way, k).start()

    def turn(c, k):
        for f in range(2):
            for way in range(2):
                near(c, f, way, k).wait_recv()
            own = part(c, f, 0, k, 0, half)
            own[...] = own[...] + (r2[c, f, 0, k] + r2[c, f, 1, k])
            if k == 0:
                far_second(c, f, 0).start()
                far_second(c, f, 1).start()
            elif k < 3:
                way = k - 1
                far_second(c, f, way).wait_recv()
                own = part(c, f, 0, k, way * quarter, quarter)
                own[...] = own[...] + r3[c, f, way]
                near_second(c, f, way).start()

    def swap(c):
        return remote(mbuf.at[c, held], relay.at[c], ts.at[c, 0], tr.at[c, 0], taker)

    def swap_on(c):
        return remote(relay.at[c], match.at[c], ts.at[c, 1], tr.at[c, 1], onward)

    def send_match(c):
        @pl.when(moves)
        def _():
            swap(c).start()

        @pl.when(jnp.logical_not(moves))
        def _():
            relay[c] = mbuf[c, held]

    def pass_match(c):
        @pl.when(moves)
        def _():
            swap(c).wait_recv()

        @pl.when(goes_on)
        def _():
            swap_on(c).start()

        @pl.when(jnp.logical_not(goes_on))
        def _():
            match[c] = relay[c]

    def finish(c):
        for f in range(2):
            for way in range(2):
                near_second(c, f, way).wait_recv()
            own = part(c, f, 0, 3, 0, half)
            own[...] = own[...] + (r4[c, f, 0] + r4[c, f, 1])
        product = pbuf.at[c, row]

        if c == 0:
            @pl.when(goes_on)
            def _():
                for e in range(chunks):
                    swap_on(e).wait_recv()

        value = product[...]
        total = None
        rest = value
        columns = jnp.concatenate([match[e] for e in range(chunks)], axis=1)
        for _ in range(3):
            top = rest.astype(jnp.bfloat16)
            rest = rest - top.astype(jnp.float32)
            add = lax.dot_general(
                columns, top, (((0,), (0,)), ((), ())), preferred_element_type=jnp.float32
            )
            total = add if total is None else total + add
        term[c] = total

        @pl.loop(1, groups)
        def _(j):
            give(c, j).start()

        for i in range(blocks):
            keep = pattern[row, group * blocks + i].astype(jnp.float32)
            rows = pl.ds(i * block, block)
            cov[rows, pl.ds(c * LANES, LANES)] = -(product[rows, :] * keep)

    def give(c, j):
        to = lax.rem(group + j, groups)
        rows = pl.ds(pl.multiple_of(to * piece, piece), piece)
        return remote(term.at[c, rows, :], dpart.at[c, j], ps.at[c, j], pr.at[c, j], peer(j))

    def mine(owner):
        return pl.ds(pl.multiple_of(owner * piece, piece), piece)

    def spread(c, j, owner):
        view = dsum.at[c, mine(owner), :]
        return remote(view, view, bs.at[c, j], br.at[c, j], peer(j))

    def settle(c):
        @pl.loop(1, groups)
        def _(j):
            give(c, j).wait_recv()

        dsum[c, mine(group), :] = (
            dinv[0, mine(group), pl.ds(c * LANES, LANES)]
            + (term[c, mine(group), :] + jnp.sum(dpart[c, pl.ds(1, groups - 1)], axis=0))
        )

        @pl.loop(1, groups)
        def _(j):
            spread(c, j, group).start()

    def collect(c):
        @pl.loop(1, groups)
        def _(j):
            spread(c, j, lax.rem(group - j + groups, groups)).wait_recv()

        diag[0, :, pl.ds(c * LANES, LANES)] = dsum[c]

    gather_begin(0)
    products(0, 0)
    for d in range(turns):
        gather_step(0, d)
        if d == turns - 2:
            gather_begin(1)
        if d > 0:
            products(0, d)
    products(0, turns)
    for k in range(4):
        send_far(0, k)
    send_match(0)
    products(1, 0)
    for k in range(4):
        gather_step(1, k)
        send_near(0, k)
        products(1, k + 1)
    pass_match(0)
    for k in range(4):
        send_far(1, k)
    send_match(1)
    for k in range(4):
        turn(0, k)
        send_near(1, k)
    pass_match(1)
    finish(0)
    for k in range(4):
        turn(1, k)
    settle(0)
    finish(1)
    collect(0)
    settle(1)
    collect(1)

    for c in range(chunks):
        leaf_own(c, leaf).wait_send()
        for way in range(2):
            for j in range(pieces):
                z_copy(c, way, j, 0).wait_send()
                leaf_copy(c, way, j, leaf).wait_send()
            for f in range(2):
                for k in range(4):
                    far(c, f, way, k).wait_send()
                    near(c, f, way, k).wait_send()
                far_second(c, f, way).wait_send()
                near_second(c, f, way).wait_send()

        @pl.loop(1, groups)
        def _(j):
            give(c, j).wait_send()
            spread(c, j, group).wait_send()

        @pl.when(moves)
        def _():
            swap(c).wait_send()

        @pl.when(goes_on)
        def _():
            swap_on(c).wait_send()


def local(ancestor_inverse, panels, pattern, diag_inverse):
    depth, width = panels.shape
    rows_out = ancestor_inverse.shape[0]
    block = diag_inverse.shape[1]
    nz = lax.axis_size("col")
    groups = 2 * nz
    supers = pattern.shape[1]
    turned = pattern.T
    chunks = block // LANES
    half, quarter = depth // 2, depth // 4
    f32, bf16 = jnp.float32, jnp.bfloat16
    pieces = 2 * (nz // 2) - 1
    dma = pltpu.SemaphoreType.DMA
    vmem = pl.BlockSpec(memory_space=pltpu.VMEM)
    sems = [
        (chunks, 2, pieces), (chunks, 2 * pieces + 1),
        (chunks, 2, 2, 4), (chunks, 2, 2, 4), (chunks, 2, 2), (chunks, 2, 2),
        (chunks, 2), (chunks, groups), (chunks, groups),
    ]
    return tuple(pl.pallas_call(
        kernel,
        out_shape=(
            jax.ShapeDtypeStruct((rows_out, width), f32),
            jax.ShapeDtypeStruct(diag_inverse.shape, f32),
        ),
        in_specs=[pl.BlockSpec(memory_space=pltpu.SMEM), vmem, vmem, vmem],
        out_specs=(vmem, vmem),
        scratch_shapes=[
            pltpu.VMEM((chunks, supers, depth, LANES), bf16),
            pltpu.VMEM((chunks, depth, LANES), bf16),
            pltpu.VMEM((chunks, depth, LANES), bf16),
            pltpu.VMEM((chunks, supers, rows_out, LANES), f32),
            pltpu.VMEM((chunks, 2, 2, 4, quarter, LANES), f32),
            pltpu.VMEM((chunks, 2, 2, 4, half, LANES), f32),
            pltpu.VMEM((chunks, 2, 2, quarter, LANES), f32),
            pltpu.VMEM((chunks, 2, 2, half, LANES), f32),
            pltpu.VMEM((chunks, block, LANES), f32),
            pltpu.VMEM((chunks, groups, block // groups, LANES), f32),
            pltpu.VMEM((chunks, block, LANES), f32),
        ] + [dma(s) for s in sems for _ in range(2)],
        compiler_params=pltpu.CompilerParams(
            collective_id=0, has_side_effects=True, vmem_limit_bytes=58 * 2**20
        ),
        cost_estimate=pl.CostEstimate(
            flops=2 * rows_out * depth * supers * block, bytes_accessed=8 * 2**20, transcendentals=0
        ),
    )(turned, ancestor_inverse, panels, diag_inverse))


def solution(mesh):
    placed = (P(("leaf", "col"), "row"), P("row", ("leaf", "col")), P(), P("row", None, None))
    return jax.shard_map(
        local,
        mesh=mesh,
        in_specs=placed,
        out_specs=(P(("leaf", "col"), "row"), P("row", None, None)),
        check_vma=False,
    )
```

```python
import jax
import jax.numpy as jnp
from jax import lax
from jax.experimental import pallas as pl
from jax.experimental.pallas import tpu as pltpu
from jax.sharding import PartitionSpec as P

MESH = pl.DeviceIdType.MESH
SIDE = 4
LANES = 128
TOP = 32000.0
PER_NAT = 180.0
OFFSETS = (2, 1, 3, 0)


def kernel(
    pattern, a_ref, panel, dinv, cov, diag,
    mbuf, match, relay, pbuf, e1, r1, e2, r2, e3, r3, e4, r4, term, dpart, dsum,
    zs, zr, ls, lr, s1, q1, s2, q2, s3, q3, s4, q4, ts, tr, ps, pr, bs, br,
):
    nz = lax.axis_size("col")
    leaf = lax.axis_index("leaf")
    row = lax.axis_index("row")
    z = lax.axis_index("col")
    y = row // SIDE
    x = lax.rem(row, SIDE)
    groups = 2 * nz
    group = leaf * nz + z
    depth = panel.shape[0]
    block = dinv.shape[1]
    blocks = depth // block
    half = depth // 2
    quarter = depth // 4
    chunks = block // LANES
    piece = block // groups

    def peer(j):
        p = lax.rem(group + j, groups)
        return (p // nz, row, lax.rem(p, nz))

    def z_dev(step):
        return (leaf, row, lax.rem(z + step + nz, nz))

    def x_dev(step):
        return (leaf, y * SIDE + lax.rem(x + step + SIDE, SIDE), z)

    def y_dev(step):
        return (leaf, lax.rem(y + step + SIDE, SIDE) * SIDE + x, z)

    other = (1 - leaf, row, z)
    held = leaf * nz + lax.rem(z + 2 * leaf + row, nz)
    taker = (row // nz, held, z)
    turned = lax.rem(row - z - 2 * (row // nz) + 2 * nz, nz)
    giver = (row // nz, leaf * nz + turned, z)
    moves = jnp.logical_or(row // nz != leaf, held != row)
    onward = (leaf, row, turned)
    goes_on = turned != z

    def remote(src, dst, send, recv, dev):
        return pltpu.make_async_remote_copy(
            src_ref=src, dst_ref=dst, send_sem=send, recv_sem=recv,
            device_id=dev, device_id_type=MESH,
        )

    barrier = pltpu.get_barrier_semaphore()

    @pl.loop(1, groups)
    def _(j):
        pl.semaphore_signal(barrier, inc=1, device_id=peer(j), device_id_type=MESH)

    for dev in (x_dev(1), x_dev(-1), y_dev(1), y_dev(-1)):
        pl.semaphore_signal(barrier, inc=1, device_id=dev, device_id_type=MESH)

    @pl.when(moves)
    def _():
        pl.semaphore_signal(barrier, inc=1, device_id=giver, device_id_type=MESH)

    for c in range(chunks):
        for i in range(blocks):
            keep = pattern[group, row * blocks + i].astype(jnp.float32)
            rows = pl.ds(i * block, block)
            values = panel[rows, pl.ds(c * LANES, LANES)].astype(jnp.float32) * keep
            mbuf[c, group, rows, :] = values.astype(jnp.bfloat16)

    pl.semaphore_wait(barrier, groups - 1 + 4 + moves.astype(jnp.int32))

    turns = nz // 2
    pieces = 2 * turns - 1

    def z_rows(way, j):
        h = j % 2 if way == 0 else 1 - j % 2
        return pl.ds(h * half, half)

    def z_copy(c, way, j, lag):
        step = -1 if way == 0 else 1
        s = leaf * nz + lax.rem(z + step * (j // 2 + lag) + 2 * nz, nz)
        view = mbuf.at[c, s, z_rows(way, j), :]
        return remote(view, view, zs.at[c, way, j], zr.at[c, way, j], z_dev(-step))

    def leaf_copy(c, way, j, lf):
        step = -1 if way == 0 else 1
        s = lf * nz + lax.rem(z + step * (j // 2 + 1) + 2 * nz, nz)
        view = mbuf.at[c, s, z_rows(way, j), :]
        n = way * pieces + j
        return remote(view, view, ls.at[c, n], lr.at[c, n], other)

    def leaf_own(c, lf):
        view = mbuf.at[c, lf * nz + z]
        return remote(view, view, ls.at[c, 2 * pieces], lr.at[c, 2 * pieces], other)

    def gather_begin(c):
        for j in range(2):
            for way in range(2):
                z_copy(c, way, j, 0).start()
        leaf_own(c, leaf).start()

    def gather_step(c, d):
        for j in range(2 * d, min(2 * d + 2, pieces)):
            for way in range(2):
                z_copy(c, way, j, 1).wait_recv()
                if j + 2 < pieces:
                    z_copy(c, way, j + 2, 0).start()
                leaf_copy(c, way, j, leaf).start()

    def multiply(c, sa, sb):
        @pl.loop(0, a_ref.shape[0] // 256)
        def _(t):
            rows = pl.ds(pl.multiple_of(t * 256, 256), 256)
            right = jnp.concatenate([mbuf[c, sa], mbuf[c, sb]], axis=1)
            out = jnp.dot(a_ref[rows, :], right, preferred_element_type=jnp.float32)
            pbuf[c, sa, rows, :] = out[:, :LANES]
            pbuf[c, sb, rows, :] = out[:, LANES:]

    def products(c, d):
        if d == 0:
            leaf_own(c, 1 - leaf).wait_recv()
            multiply(c, leaf * nz + z, (1 - leaf) * nz + z)
            return
        for j in range(2 * d - 2, min(2 * d, pieces)):
            for way in range(2):
                leaf_copy(c, way, j, 1 - leaf).wait_recv()
        up = lax.rem(z + d, nz)
        down = lax.rem(z + nz - d, nz)
        if d == turns:
            multiply(c, leaf * nz + up, (1 - leaf) * nz + up)
        else:
            multiply(c, leaf * nz + up, leaf * nz + down)
            multiply(c, (1 - leaf) * nz + up, (1 - leaf) * nz + down)

    def first(f):
        return (x, y)[f]

    def second(f):
        return (y, x)[f]

    def dev_first(f, step):
        return (x_dev, y_dev)[f](step)

    def dev_second(f, step):
        return (y_dev, x_dev)[f](step)

    def part(c, f, df, k, lo, n):
        a = lax.rem(first(f) + df, SIDE)
        b = lax.rem(second(f) + OFFSETS[k], SIDE)
        s = b * SIDE + a if f == 0 else a * SIDE + b
        return pbuf.at[c, s, pl.ds(f * half + lo, n), :]

    def encode(to, value):
        n = value.shape[0]
        shaped = value.reshape(2, n // 16, 8, LANES)
        largest = jnp.max(jnp.abs(shaped), axis=1).reshape(16, LANES)
        level = jnp.ceil(jnp.log(jnp.maximum(largest, 1e-30)) * PER_NAT)
        to[pl.ds(0, 16), :] = level.astype(jnp.int32).astype(jnp.int16)
        factor = (TOP * jnp.exp(level * (-1.0 / PER_NAT))).reshape(2, 1, 8, LANES)
        rounded = jnp.round(shaped * factor).reshape(n, LANES)
        to[pl.ds(16, n), :] = rounded.astype(jnp.int32).astype(jnp.int16)

    def decode(at):
        n = at.shape[0] - 16
        level = at[pl.ds(0, 16), :].astype(jnp.int32).astype(jnp.float32)
        factor = (jnp.exp(level * (1.0 / PER_NAT)) * (1.0 / TOP)).reshape(2, 1, 8, LANES)
        value = at[pl.ds(16, n), :].astype(jnp.int32).astype(jnp.float32)
        return (value.reshape(2, n // 16, 8, LANES) * factor).reshape(n, LANES)

    def far(c, f, way, k):
        return remote(
            e1.at[c, f, way, k], r1.at[c, f, way, k],
            s1.at[c, f, way, k], q1.at[c, f, way, k], dev_first(f, 1 - 2 * way),
        )

    def near(c, f, way, k):
        return remote(
            e2.at[c, f, way, k], r2.at[c, f, way, k],
            s2.at[c, f, way, k], q2.at[c, f, way, k], dev_first(f, 1 - 2 * way),
        )

    def far_second(c, f, way):
        return remote(
            e3.at[c, f, way], r3.at[c, f, way],
            s3.at[c, f, way], q3.at[c, f, way], dev_second(f, 1 - 2 * way),
        )

    def near_second(c, f, way):
        return remote(
            e4.at[c, f, way], r4.at[c, f, way],
            s4.at[c, f, way], q4.at[c, f, way], dev_second(f, 1 - 2 * way),
        )

    def joined(value, add, way):
        low, high = value[:quarter], value[quarter:]
        return jnp.concatenate([low + add, high] if way == 0 else [low, high + add], axis=0)

    def send_far(c, k):
        for f in range(2):
            for way in range(2):
                encode(e1.at[c, f, way, k], part(c, f, 2, k, way * quarter, quarter)[...])
                far(c, f, way, k).start()

    def send_near(c, k):
        for f in range(2):
            for way in range(2):
                far(c, f, way, k).wait_recv()
                own = part(c, f, 1 + 2 * way, k, 0, half)[...]
                encode(e2.at[c, f, way, k], joined(own, decode(r1.at[c, f, way, k]), way))
                near(c, f, way, k).start()

    def turn(c, k):
        for f in range(2):
            for way in range(2):
                near(c, f, way, k).wait_recv()
            own = part(c, f, 0, k, 0, half)
            total = own[...] + (decode(r2.at[c, f, 0, k]) + decode(r2.at[c, f, 1, k]))
            if k == 0:
                for way in range(2):
                    encode(e3.at[c, f, way], total[way * quarter:(way + 1) * quarter])
                    far_second(c, f, way).start()
            elif k < 3:
                way = k - 1
                far_second(c, f, way).wait_recv()
                encode(e4.at[c, f, way], joined(total, decode(r3.at[c, f, way]), way))
                near_second(c, f, way).start()
            else:
                own[...] = total

    def swap(c):
        return remote(mbuf.at[c, held], relay.at[c], ts.at[c, 0], tr.at[c, 0], taker)

    def swap_on(c):
        return remote(relay.at[c], match.at[c], ts.at[c, 1], tr.at[c, 1], onward)

    def send_match(c):
        @pl.when(moves)
        def _():
            swap(c).start()

        @pl.when(jnp.logical_not(moves))
        def _():
            relay[c] = mbuf[c, held]

    def pass_match(c):
        @pl.when(moves)
        def _():
            swap(c).wait_recv()

        @pl.when(goes_on)
        def _():
            swap_on(c).start()

        @pl.when(jnp.logical_not(goes_on))
        def _():
            match[c] = relay[c]

    def finish(c):
        for f in range(2):
            for way in range(2):
                near_second(c, f, way).wait_recv()
            own = part(c, f, 0, 3, 0, half)
            own[...] = own[...] + (decode(r4.at[c, f, 0]) + decode(r4.at[c, f, 1]))
        product = pbuf.at[c, row]

        if c == 0:
            @pl.when(goes_on)
            def _():
                for e in range(chunks):
                    swap_on(e).wait_recv()

        value = product[...]
        total = None
        rest = value
        columns = jnp.concatenate([match[e] for e in range(chunks)], axis=1)
        for _ in range(3):
            top = rest.astype(jnp.bfloat16)
            rest = rest - top.astype(jnp.float32)
            add = lax.dot_general(
                columns, top, (((0,), (0,)), ((), ())), preferred_element_type=jnp.float32
            )
            total = add if total is None else total + add
        term[c] = total

        @pl.loop(1, groups)
        def _(j):
            give(c, j).start()

        for i in range(blocks):
            keep = pattern[row, group * blocks + i].astype(jnp.float32)
            rows = pl.ds(i * block, block)
            cov[rows, pl.ds(c * LANES, LANES)] = -(product[rows, :] * keep)

    def give(c, j):
        to = lax.rem(group + j, groups)
        rows = pl.ds(pl.multiple_of(to * piece, piece), piece)
        return remote(term.at[c, rows, :], dpart.at[c, j], ps.at[c, j], pr.at[c, j], peer(j))

    def mine(owner):
        return pl.ds(pl.multiple_of(owner * piece, piece), piece)

    def spread(c, j, owner):
        view = dsum.at[c, mine(owner), :]
        return remote(view, view, bs.at[c, j], br.at[c, j], peer(j))

    def settle(c):
        @pl.loop(1, groups)
        def _(j):
            give(c, j).wait_recv()

        dsum[c, mine(group), :] = (
            dinv[0, mine(group), pl.ds(c * LANES, LANES)]
            + (term[c, mine(group), :] + jnp.sum(dpart[c, pl.ds(1, groups - 1)], axis=0))
        )

        @pl.loop(1, groups)
        def _(j):
            spread(c, j, group).start()

    def collect(c):
        @pl.loop(1, groups)
        def _(j):
            spread(c, j, lax.rem(group - j + groups, groups)).wait_recv()

        diag[0, :, pl.ds(c * LANES, LANES)] = dsum[c]

    gather_begin(0)
    products(0, 0)
    for d in range(turns):
        gather_step(0, d)
        if d == turns - 2:
            gather_begin(1)
        if d > 0:
            products(0, d)
    products(0, turns)
    for k in range(4):
        send_far(0, k)
    send_match(0)
    products(1, 0)
    for k in range(4):
        gather_step(1, k)
        send_near(0, k)
        products(1, k + 1)
    pass_match(0)
    for k in range(4):
        send_far(1, k)
    send_match(1)
    for k in range(4):
        turn(0, k)
        send_near(1, k)
    pass_match(1)
    finish(0)
    for k in range(4):
        turn(1, k)
    settle(0)
    finish(1)
    collect(0)
    settle(1)
    collect(1)

    for c in range(chunks):
        leaf_own(c, leaf).wait_send()
        for way in range(2):
            for j in range(pieces):
                z_copy(c, way, j, 0).wait_send()
                leaf_copy(c, way, j, leaf).wait_send()
            for f in range(2):
                for k in range(4):
                    far(c, f, way, k).wait_send()
                    near(c, f, way, k).wait_send()
                far_second(c, f, way).wait_send()
                near_second(c, f, way).wait_send()

        @pl.loop(1, groups)
        def _(j):
            give(c, j).wait_send()
            spread(c, j, group).wait_send()

        @pl.when(moves)
        def _():
            swap(c).wait_send()

        @pl.when(goes_on)
        def _():
            swap_on(c).wait_send()


def local(ancestor_inverse, panels, pattern, diag_inverse):
    depth, width = panels.shape
    rows_out = ancestor_inverse.shape[0]
    block = diag_inverse.shape[1]
    nz = lax.axis_size("col")
    groups = 2 * nz
    supers = pattern.shape[1]
    turned = pattern.T
    chunks = block // LANES
    half, quarter = depth // 2, depth // 4
    f32, bf16 = jnp.float32, jnp.bfloat16
    pieces = 2 * (nz // 2) - 1
    dma = pltpu.SemaphoreType.DMA
    vmem = pl.BlockSpec(memory_space=pltpu.VMEM)
    sums = [
        (chunks, 2, 2, 4, quarter + 16, LANES), (chunks, 2, 2, 4, half + 16, LANES),
        (chunks, 2, 2, quarter + 16, LANES), (chunks, 2, 2, half + 16, LANES),
    ]
    sems = [
        (chunks, 2, pieces), (chunks, 2 * pieces + 1),
        (chunks, 2, 2, 4), (chunks, 2, 2, 4), (chunks, 2, 2), (chunks, 2, 2),
        (chunks, 2), (chunks, groups), (chunks, groups),
    ]
    return tuple(pl.pallas_call(
        kernel,
        out_shape=(
            jax.ShapeDtypeStruct((rows_out, width), f32),
            jax.ShapeDtypeStruct(diag_inverse.shape, f32),
        ),
        in_specs=[pl.BlockSpec(memory_space=pltpu.SMEM), vmem, vmem, vmem],
        out_specs=(vmem, vmem),
        scratch_shapes=[
            pltpu.VMEM((chunks, supers, depth, LANES), bf16),
            pltpu.VMEM((chunks, depth, LANES), bf16),
            pltpu.VMEM((chunks, depth, LANES), bf16),
            pltpu.VMEM((chunks, supers, rows_out, LANES), f32),
        ] + [pltpu.VMEM(s, jnp.int16) for s in sums for _ in range(2)] + [
            pltpu.VMEM((chunks, block, LANES), f32),
            pltpu.VMEM((chunks, groups, block // groups, LANES), f32),
            pltpu.VMEM((chunks, block, LANES), f32),
        ] + [dma(s) for s in sems for _ in range(2)],
        compiler_params=pltpu.CompilerParams(
            collective_id=0, has_side_effects=True, vmem_limit_bytes=58 * 2**20
        ),
        cost_estimate=pl.CostEstimate(
            flops=2 * rows_out * depth * supers * block, bytes_accessed=8 * 2**20, transcendentals=0
        ),
    )(turned, ancestor_inverse, panels, diag_inverse))


def solution(mesh):
    placed = (P(("leaf", "col"), "row"), P("row", ("leaf", "col")), P(), P("row", None, None))
    return jax.shard_map(
        local,
        mesh=mesh,
        in_specs=placed,
        out_specs=(P(("leaf", "col"), "row"), P("row", None, None)),
        check_vma=False,
    )
```

```python
import jax
import jax.numpy as jnp
from jax import lax
from jax.experimental import pallas as pl
from jax.experimental.pallas import tpu as pltpu
from jax.sharding import PartitionSpec as P

MESH = pl.DeviceIdType.MESH
SIDE = 4
LANES = 128
TOP = 32000.0
PER_NAT = 180.0
OFFSETS = (2, 1, 3, 0)


def kernel(
    pattern, a_ref, panel, dinv, cov, diag,
    mbuf, match, relay, pbuf, e1, r1, e2, r2, e3, r3, e4, r4, term, traded, dpart, dsum,
    zs, zr, ls, lr, s1, q1, s2, q2, s3, q3, s4, q4, ts, tr, ds, dr, ps, pr, bs, br,
):
    nz = lax.axis_size("col")
    leaf = lax.axis_index("leaf")
    row = lax.axis_index("row")
    z = lax.axis_index("col")
    y = row // SIDE
    x = lax.rem(row, SIDE)
    groups = 2 * nz
    group = leaf * nz + z
    depth = panel.shape[0]
    block = dinv.shape[1]
    blocks = depth // block
    half = depth // 2
    quarter = depth // 4
    chunks = block // LANES
    piece = block // groups

    def z_dev(step):
        return (leaf, row, lax.rem(z + step + nz, nz))

    def x_dev(step):
        return (leaf, y * SIDE + lax.rem(x + step + SIDE, SIDE), z)

    def y_dev(step):
        return (leaf, lax.rem(y + step + SIDE, SIDE) * SIDE + x, z)

    other = (1 - leaf, row, z)
    held = leaf * nz + lax.rem(z + 2 * leaf + row, nz)
    taker = (row // nz, held, z)
    turned = lax.rem(row - z - 2 * (row // nz) + 2 * nz, nz)
    giver = (row // nz, leaf * nz + turned, z)
    moves = jnp.logical_or(row // nz != leaf, held != row)
    onward = (leaf, row, turned)
    goes_on = turned != z

    def remote(src, dst, send, recv, dev):
        return pltpu.make_async_remote_copy(
            src_ref=src, dst_ref=dst, send_sem=send, recv_sem=recv,
            device_id=dev, device_id_type=MESH,
        )

    barrier = pltpu.get_barrier_semaphore()

    @pl.loop(1, nz)
    def _(j):
        pl.semaphore_signal(barrier, inc=1, device_id=z_dev(j), device_id_type=MESH)

    for dev in (other, x_dev(1), x_dev(-1), y_dev(1), y_dev(-1)):
        pl.semaphore_signal(barrier, inc=1, device_id=dev, device_id_type=MESH)

    @pl.when(moves)
    def _():
        pl.semaphore_signal(barrier, inc=1, device_id=giver, device_id_type=MESH)

    for c in range(chunks):
        for i in range(blocks):
            keep = pattern[group, row * blocks + i].astype(jnp.float32)
            rows = pl.ds(i * block, block)
            values = panel[rows, pl.ds(c * LANES, LANES)].astype(jnp.float32) * keep
            mbuf[c, group, rows, :] = values.astype(jnp.bfloat16)

    pl.semaphore_wait(barrier, nz + 4 + moves.astype(jnp.int32))

    turns = nz // 2
    pieces = 2 * turns - 1

    def z_rows(way, j):
        h = j % 2 if way == 0 else 1 - j % 2
        return pl.ds(h * half, half)

    def z_copy(c, way, j, lag):
        step = -1 if way == 0 else 1
        s = leaf * nz + lax.rem(z + step * (j // 2 + lag) + 2 * nz, nz)
        view = mbuf.at[c, s, z_rows(way, j), :]
        return remote(view, view, zs.at[c, way, j], zr.at[c, way, j], z_dev(-step))

    def leaf_copy(c, way, j, lf):
        step = -1 if way == 0 else 1
        s = lf * nz + lax.rem(z + step * (j // 2 + 1) + 2 * nz, nz)
        view = mbuf.at[c, s, z_rows(way, j), :]
        n = way * pieces + j
        return remote(view, view, ls.at[c, n], lr.at[c, n], other)

    def leaf_own(c, lf):
        view = mbuf.at[c, lf * nz + z]
        return remote(view, view, ls.at[c, 2 * pieces], lr.at[c, 2 * pieces], other)

    def gather_begin(c):
        for j in range(2):
            for way in range(2):
                z_copy(c, way, j, 0).start()
        leaf_own(c, leaf).start()

    def gather_step(c, d):
        for j in range(2 * d, min(2 * d + 2, pieces)):
            for way in range(2):
                z_copy(c, way, j, 1).wait_recv()
                if j + 2 < pieces:
                    z_copy(c, way, j + 2, 0).start()
                leaf_copy(c, way, j, leaf).start()

    def multiply(c, sa, sb):
        right = jnp.concatenate([mbuf[c, sa], mbuf[c, sb]], axis=1)
        out = jnp.dot(a_ref[...], right, preferred_element_type=jnp.float32)
        pbuf[c, sa] = out[:, :LANES]
        pbuf[c, sb] = out[:, LANES:]

    def products(c, d):
        if d == 0:
            leaf_own(c, 1 - leaf).wait_recv()
            multiply(c, leaf * nz + z, (1 - leaf) * nz + z)
            return
        for j in range(2 * d - 2, min(2 * d, pieces)):
            for way in range(2):
                leaf_copy(c, way, j, 1 - leaf).wait_recv()
        up = lax.rem(z + d, nz)
        down = lax.rem(z + nz - d, nz)
        if d == turns:
            multiply(c, leaf * nz + up, (1 - leaf) * nz + up)
        else:
            multiply(c, leaf * nz + up, leaf * nz + down)
            multiply(c, (1 - leaf) * nz + up, (1 - leaf) * nz + down)

    def first(f):
        return (x, y)[f]

    def second(f):
        return (y, x)[f]

    def dev_first(f, step):
        return (x_dev, y_dev)[f](step)

    def dev_second(f, step):
        return (y_dev, x_dev)[f](step)

    def quarter_of(c, s, f, q):
        return pbuf.at[c, s, pl.ds(pl.multiple_of(f * half + q * quarter, quarter), quarter), :]

    def own_block(f, k):
        t = lax.rem(second(f) + OFFSETS[k], SIDE)
        return t, (t * SIDE + x if f == 0 else y * SIDE + t)

    def place(f, s):
        a, b = (lax.rem(s, SIDE), s // SIDE)[::1 - 2 * f]
        return lax.rem(a - first(f) + SIDE, SIDE), b

    def encode(to, value):
        n = value.shape[0]
        shaped = value.reshape(2, n // 16, 8, LANES)
        largest = jnp.max(jnp.abs(shaped), axis=1).reshape(16, LANES)
        level = jnp.ceil(jnp.log(jnp.maximum(largest, 1e-30)) * PER_NAT)
        to[pl.ds(0, 16), :] = level.astype(jnp.int32).astype(jnp.int16)
        factor = (TOP * jnp.exp(level * (-1.0 / PER_NAT))).reshape(2, 1, 8, LANES)
        rounded = jnp.round(shaped * factor).reshape(n, LANES)
        to[pl.ds(16, n), :] = rounded.astype(jnp.int32).astype(jnp.int16)

    def decode(at):
        n = at.shape[0] - 16
        level = at[pl.ds(0, 16), :].astype(jnp.int32).astype(jnp.float32)
        factor = (jnp.exp(level * (1.0 / PER_NAT)) * (1.0 / TOP)).reshape(2, 1, 8, LANES)
        value = at[pl.ds(16, n), :].astype(jnp.int32).astype(jnp.float32)
        return (value.reshape(2, n // 16, 8, LANES) * factor).reshape(n, LANES)

    def far(c, f, way, t):
        return remote(
            e1.at[c, f, way, t], r1.at[c, f, way, t],
            s1.at[c, f, way, t], q1.at[c, f, way, t], dev_first(f, 1 - 2 * way),
        )

    def near(c, f, way, t):
        return remote(
            e2.at[c, f, way, t], r2.at[c, f, way, t],
            s2.at[c, f, way, t], q2.at[c, f, way, t], dev_first(f, 1 - 2 * way),
        )

    def far_second(c, f, way):
        return remote(
            e3.at[c, f, way], r3.at[c, f, way],
            s3.at[c, f, way], q3.at[c, f, way], dev_second(f, 1 - 2 * way),
        )

    def near_second(c, f, way):
        return remote(
            e4.at[c, f, way], r4.at[c, f, way],
            s4.at[c, f, way], q4.at[c, f, way], dev_second(f, 1 - 2 * way),
        )

    def arrived(d, act):
        both = 1 if d in (0, turns) else 2

        @pl.loop(0, 2 * both)
        def _(i):
            step = d if both == 1 else d * (1 - 2 * lax.rem(i, 2))
            act((i // both) * nz + lax.rem(z + step + nz, nz))

    def send_far(c, d):
        def act(s):
            for f in range(2):
                ahead, t = place(f, s)

                @pl.when(ahead == 2)
                def _():
                    for way in range(2):
                        encode(e1.at[c, f, way, t], quarter_of(c, s, f, way)[...])
                        far(c, f, way, t).start()

        arrived(d, act)

    def send_near(c, k):
        for f in range(2):
            t = lax.rem(second(f) + OFFSETS[k], SIDE)
            for way in range(2):
                a = lax.rem(first(f) + 1 + 2 * way, SIDE)
                s = t * SIDE + a if f == 0 else a * SIDE + t
                encode(e2.at[c, f, way, t, 1 - way], quarter_of(c, s, f, 1 - way)[...])
                far(c, f, way, t).wait_recv()
                value = quarter_of(c, s, f, way)[...] + decode(r1.at[c, f, way, t])
                encode(e2.at[c, f, way, t, way], value)
                near(c, f, way, t).start()

    def turn(c, k):
        for f in range(2):
            t, s = own_block(f, k)
            for way in range(2):
                near(c, f, way, t).wait_recv()
            for q in range(2):
                own = quarter_of(c, s, f, q)
                own[...] = own[...] + (decode(r2.at[c, f, 0, t, q]) + decode(r2.at[c, f, 1, t, q]))
            if k == 0:
                for way in range(2):
                    encode(e3.at[c, f, way], quarter_of(c, s, f, way)[...])
                    far_second(c, f, way).start()
            elif k < 3:
                way = k - 1
                encode(e4.at[c, f, way, 1 - way], quarter_of(c, s, f, 1 - way)[...])
                far_second(c, f, way).wait_recv()
                value = quarter_of(c, s, f, way)[...] + decode(r3.at[c, f, way])
                encode(e4.at[c, f, way, way], value)
                near_second(c, f, way).start()

    def swap(c):
        return remote(mbuf.at[c, held], relay.at[c], ts.at[c, 0], tr.at[c, 0], taker)

    def swap_on(c):
        return remote(relay.at[c], match.at[c], ts.at[c, 1], tr.at[c, 1], onward)

    def send_match(c):
        @pl.when(moves)
        def _():
            swap(c).start()

        @pl.when(jnp.logical_not(moves))
        def _():
            relay[c] = mbuf[c, held]

    def pass_match(c):
        @pl.when(moves)
        def _():
            swap(c).wait_recv()

        @pl.when(goes_on)
        def _():
            swap_on(c).start()

        @pl.when(jnp.logical_not(goes_on))
        def _():
            match[c] = relay[c]

    def finish(c):
        for f in range(2):
            for way in range(2):
                near_second(c, f, way).wait_recv()
            for q in range(2):
                own = quarter_of(c, row, f, q)
                own[...] = own[...] + (decode(r4.at[c, f, 0, q]) + decode(r4.at[c, f, 1, q]))
        product = pbuf.at[c, row]
        for i in range(blocks):
            keep = pattern[row, group * blocks + i].astype(jnp.float32)
            rows = pl.ds(i * block, block)
            cov[rows, pl.ds(c * LANES, LANES)] = -(product[rows, :] * keep)

    def diag_terms():
        @pl.when(goes_on)
        def _():
            for c in range(chunks):
                swap_on(c).wait_recv()

        columns = jnp.concatenate([match[c] for c in range(chunks)], axis=1)
        rest = jnp.concatenate([pbuf[c, row] for c in range(chunks)], axis=1)
        total = None
        for _ in range(3):
            top = rest.astype(jnp.bfloat16)
            rest = rest - top.astype(jnp.float32)
            add = lax.dot_general(
                columns, top, (((0,), (0,)), ((), ())), preferred_element_type=jnp.float32
            )
            total = add if total is None else total + add
        term[...] = total

    wide = block // 2

    def side(lf):
        return pl.ds(pl.multiple_of(lf * wide, wide), wide)

    def mine(owner):
        return pl.ds(pl.multiple_of(leaf * wide + owner * piece, piece), piece)

    def trade():
        return remote(term.at[side(1 - leaf), :], traded, ds.at[0], dr.at[0], other)

    def give(j):
        return remote(
            term.at[mine(lax.rem(z + j, nz)), :], dpart.at[j], ps.at[j], pr.at[j], z_dev(j)
        )

    def spread(j, owner):
        view = dsum.at[mine(owner), :]
        return remote(view, view, bs.at[j], br.at[j], z_dev(j))

    def hand(lf):
        view = dsum.at[side(lf), :]
        return remote(view, view, ds.at[1], dr.at[1], other)

    def diag_sum():
        trade().start()
        trade().wait_recv()
        term[side(leaf), :] = term[side(leaf), :] + traded[...]

        @pl.loop(1, nz)
        def _(j):
            give(j).start()

        @pl.loop(1, nz)
        def _(j):
            give(j).wait_recv()

        dsum[mine(z), :] = dinv[0, mine(z), :] + (
            term[mine(z), :] + jnp.sum(dpart[pl.ds(1, nz - 1)], axis=0)
        )

        @pl.loop(1, nz)
        def _(j):
            spread(j, z).start()

        @pl.loop(1, nz)
        def _(j):
            spread(j, lax.rem(z - j + nz, nz)).wait_recv()

        hand(leaf).start()
        hand(1 - leaf).wait_recv()
        diag[0] = dsum[...]

    gather_begin(0)
    for d in range(turns):
        gather_step(0, d)
        if d == turns - 2:
            gather_begin(1)
        products(0, d)
        send_far(0, d)
    products(0, turns)
    send_far(0, turns)
    send_match(0)
    for d in range(turns):
        gather_step(1, d)
        send_near(0, d)
        products(1, d)
        send_far(1, d)
    products(1, turns)
    send_far(1, turns)
    send_match(1)
    pass_match(0)
    for k in range(SIDE):
        turn(0, k)
        send_near(1, k)
    finish(0)
    pass_match(1)
    for k in range(SIDE):
        turn(1, k)
    finish(1)
    diag_terms()
    diag_sum()

    for c in range(chunks):
        leaf_own(c, leaf).wait_send()
        for way in range(2):
            for j in range(pieces):
                z_copy(c, way, j, 0).wait_send()
                leaf_copy(c, way, j, leaf).wait_send()
            for f in range(2):
                for k in range(4):
                    far(c, f, way, k).wait_send()
                    near(c, f, way, k).wait_send()
                far_second(c, f, way).wait_send()
                near_second(c, f, way).wait_send()

        @pl.when(moves)
        def _():
            swap(c).wait_send()

        @pl.when(goes_on)
        def _():
            swap_on(c).wait_send()

    trade().wait_send()
    hand(leaf).wait_send()

    @pl.loop(1, nz)
    def _(j):
        give(j).wait_send()
        spread(j, z).wait_send()


def local(ancestor_inverse, panels, pattern, diag_inverse):
    depth, width = panels.shape
    rows_out = ancestor_inverse.shape[0]
    block = diag_inverse.shape[1]
    nz = lax.axis_size("col")
    groups = 2 * nz
    supers = pattern.shape[1]
    turned = pattern.T
    chunks = block // LANES
    half, quarter = depth // 2, depth // 4
    f32, bf16 = jnp.float32, jnp.bfloat16
    pieces = 2 * (nz // 2) - 1
    dma = pltpu.SemaphoreType.DMA
    vmem = pl.BlockSpec(memory_space=pltpu.VMEM)
    sums = [
        (chunks, 2, 2, 4, quarter + 16, LANES), (chunks, 2, 2, 4, 2, quarter + 16, LANES),
        (chunks, 2, 2, quarter + 16, LANES), (chunks, 2, 2, 2, quarter + 16, LANES),
    ]
    sems = [
        (chunks, 2, pieces), (chunks, 2 * pieces + 1),
        (chunks, 2, 2, 4), (chunks, 2, 2, 4), (chunks, 2, 2), (chunks, 2, 2),
        (chunks, 2), (2,), (nz,), (nz,),
    ]
    return tuple(pl.pallas_call(
        kernel,
        out_shape=(
            jax.ShapeDtypeStruct((rows_out, width), f32),
            jax.ShapeDtypeStruct(diag_inverse.shape, f32),
        ),
        in_specs=[pl.BlockSpec(memory_space=pltpu.SMEM), vmem, vmem, vmem],
        out_specs=(vmem, vmem),
        scratch_shapes=[
            pltpu.VMEM((chunks, supers, depth, LANES), bf16),
            pltpu.VMEM((chunks, depth, LANES), bf16),
            pltpu.VMEM((chunks, depth, LANES), bf16),
            pltpu.VMEM((chunks, supers, rows_out, LANES), f32),
        ] + [pltpu.VMEM(s, jnp.int16) for s in sums for _ in range(2)] + [
            pltpu.VMEM((block, block), f32),
            pltpu.VMEM((block // 2, block), f32),
            pltpu.VMEM((nz, block // groups, block), f32),
            pltpu.VMEM((block, block), f32),
        ] + [dma(s) for s in sems for _ in range(2)],
        compiler_params=pltpu.CompilerParams(
            collective_id=0, has_side_effects=True, vmem_limit_bytes=58 * 2**20
        ),
        cost_estimate=pl.CostEstimate(
            flops=2 * rows_out * depth * supers * block, bytes_accessed=8 * 2**20, transcendentals=0
        ),
    )(turned, ancestor_inverse, panels, diag_inverse))


def solution(mesh):
    placed = (P(("leaf", "col"), "row"), P("row", ("leaf", "col")), P(), P("row", None, None))
    return jax.shard_map(
        local,
        mesh=mesh,
        in_specs=placed,
        out_specs=(P(("leaf", "col"), "row"), P("row", None, None)),
        check_vma=False,
    )
```

```python
import jax
import jax.numpy as jnp
from jax import lax
from jax.experimental import pallas as pl
from jax.experimental.pallas import tpu as pltpu
from jax.sharding import PartitionSpec as P

MESH = pl.DeviceIdType.MESH
SIDE = 4
LANES = 128
TOP = 32000.0
PER_NAT = 180.0
OFFSETS = (2, 1, 3, 0)


def kernel(
    pattern, a_ref, panel, dinv, cov, diag,
    mbuf, match, relay, pbuf, e1, r1, e2, r2, e3, r3, e4, r4, term, traded, dpart, dsum,
    zs, zr, ls, lr, s1, q1, s2, q2, s3, q3, s4, q4, ts, tr, ds, dr, ps, pr, bs, br,
):
    nz = lax.axis_size("col")
    leaf = lax.axis_index("leaf")
    row = lax.axis_index("row")
    z = lax.axis_index("col")
    y = row // SIDE
    x = lax.rem(row, SIDE)
    groups = 2 * nz
    group = leaf * nz + z
    depth = panel.shape[0]
    block = dinv.shape[1]
    blocks = depth // block
    half = depth // 2
    quarter = depth // 4
    chunks = block // LANES
    piece = block // groups

    def z_dev(step):
        return (leaf, row, lax.rem(z + step + nz, nz))

    def x_dev(step):
        return (leaf, y * SIDE + lax.rem(x + step + SIDE, SIDE), z)

    def y_dev(step):
        return (leaf, lax.rem(y + step + SIDE, SIDE) * SIDE + x, z)

    other = (1 - leaf, row, z)
    held = leaf * nz + lax.rem(z + 2 * leaf + row, nz)
    taker = (row // nz, held, z)
    turned = lax.rem(row - z - 2 * (row // nz) + 2 * nz, nz)
    giver = (row // nz, leaf * nz + turned, z)
    moves = jnp.logical_or(row // nz != leaf, held != row)
    onward = (leaf, row, turned)
    goes_on = turned != z

    def remote(src, dst, send, recv, dev):
        return pltpu.make_async_remote_copy(
            src_ref=src, dst_ref=dst, send_sem=send, recv_sem=recv,
            device_id=dev, device_id_type=MESH,
        )

    barrier = pltpu.get_barrier_semaphore()

    @pl.loop(1, nz)
    def _(j):
        pl.semaphore_signal(barrier, inc=1, device_id=z_dev(j), device_id_type=MESH)

    for dev in (other, x_dev(1), x_dev(-1), y_dev(1), y_dev(-1)):
        pl.semaphore_signal(barrier, inc=1, device_id=dev, device_id_type=MESH)

    @pl.when(moves)
    def _():
        pl.semaphore_signal(barrier, inc=1, device_id=giver, device_id_type=MESH)

    for c in range(chunks):
        for i in range(blocks):
            keep = pattern[group, row * blocks + i].astype(jnp.float32)
            rows = pl.ds(i * block, block)
            values = panel[rows, pl.ds(c * LANES, LANES)].astype(jnp.float32) * keep
            mbuf[c, group, rows, :] = values.astype(jnp.bfloat16)

    pl.semaphore_wait(barrier, nz + 4 + moves.astype(jnp.int32))

    turns = nz // 2
    pieces = 2 * turns - 1

    def z_rows(way, j):
        h = j % 2 if way == 0 else 1 - j % 2
        return pl.ds(h * half, half)

    def z_copy(c, way, j, lag):
        step = -1 if way == 0 else 1
        s = leaf * nz + lax.rem(z + step * (j // 2 + lag) + 2 * nz, nz)
        view = mbuf.at[c, s, z_rows(way, j), :]
        return remote(view, view, zs.at[c, way, j], zr.at[c, way, j], z_dev(-step))

    def leaf_copy(c, way, j, lf):
        step = -1 if way == 0 else 1
        s = lf * nz + lax.rem(z + step * (j // 2 + 1) + 2 * nz, nz)
        view = mbuf.at[c, s, z_rows(way, j), :]
        n = way * pieces + j
        return remote(view, view, ls.at[c, n], lr.at[c, n], other)

    def leaf_own(c, lf):
        view = mbuf.at[c, lf * nz + z]
        return remote(view, view, ls.at[c, 2 * pieces], lr.at[c, 2 * pieces], other)

    def gather_begin(c):
        for j in range(2):
            for way in range(2):
                z_copy(c, way, j, 0).start()
        leaf_own(c, leaf).start()

    def gather_step(c, d):
        for j in range(2 * d, min(2 * d + 2, pieces)):
            for way in range(2):
                z_copy(c, way, j, 1).wait_recv()
                if j + 2 < pieces:
                    z_copy(c, way, j + 2, 0).start()
                leaf_copy(c, way, j, leaf).start()

    def multiply(c, sa, sb):
        right = jnp.concatenate([mbuf[c, sa], mbuf[c, sb]], axis=1)
        out = jnp.dot(a_ref[...], right, preferred_element_type=jnp.float32)
        pbuf[c, sa] = out[:, :LANES]
        pbuf[c, sb] = out[:, LANES:]

    def products(c, d):
        if d == 0:
            leaf_own(c, 1 - leaf).wait_recv()
            multiply(c, leaf * nz + z, (1 - leaf) * nz + z)
            return
        for j in range(2 * d - 2, min(2 * d, pieces)):
            for way in range(2):
                leaf_copy(c, way, j, 1 - leaf).wait_recv()
        up = lax.rem(z + d, nz)
        down = lax.rem(z + nz - d, nz)
        if d == turns:
            multiply(c, leaf * nz + up, (1 - leaf) * nz + up)
        else:
            multiply(c, leaf * nz + up, leaf * nz + down)
            multiply(c, (1 - leaf) * nz + up, (1 - leaf) * nz + down)

    def first(f):
        return (x, y)[f]

    def second(f):
        return (y, x)[f]

    def dev_first(f, step):
        return (x_dev, y_dev)[f](step)

    def dev_second(f, step):
        return (y_dev, x_dev)[f](step)

    def quarter_of(c, s, f, q):
        return pbuf.at[c, s, pl.ds(pl.multiple_of(f * half + q * quarter, quarter), quarter), :]

    def own_block(f, k):
        t = lax.rem(second(f) + OFFSETS[k], SIDE)
        return t, (t * SIDE + x if f == 0 else y * SIDE + t)

    def place(f, s):
        a, b = (lax.rem(s, SIDE), s // SIDE)[::1 - 2 * f]
        return lax.rem(a - first(f) + SIDE, SIDE), b

    def encode(to, value):
        n = value.shape[0]
        shaped = value.reshape(2, n // 16, 8, LANES)
        largest = jnp.max(jnp.abs(shaped), axis=1).reshape(16, LANES)
        level = jnp.ceil(jnp.log(jnp.maximum(largest, 1e-30)) * PER_NAT)
        to[pl.ds(0, 16), :] = level.astype(jnp.int32).astype(jnp.int16)
        factor = (TOP * jnp.exp(level * (-1.0 / PER_NAT))).reshape(2, 1, 8, LANES)
        rounded = jnp.round(shaped * factor).reshape(n, LANES)
        to[pl.ds(16, n), :] = rounded.astype(jnp.int32).astype(jnp.int16)

    def decode(at):
        n = at.shape[0] - 16
        level = at[pl.ds(0, 16), :].astype(jnp.int32).astype(jnp.float32)
        factor = (jnp.exp(level * (1.0 / PER_NAT)) * (1.0 / TOP)).reshape(2, 1, 8, LANES)
        value = at[pl.ds(16, n), :].astype(jnp.int32).astype(jnp.float32)
        return (value.reshape(2, n // 16, 8, LANES) * factor).reshape(n, LANES)

    def far(c, f, way, t):
        return remote(
            e1.at[c, f, way, t], r1.at[c, f, way, t],
            s1.at[c, f, way, t], q1.at[c, f, way, t], dev_first(f, 1 - 2 * way),
        )

    def near(c, f, way, t):
        return remote(
            e2.at[c, f, way, t], r2.at[c, f, way, t],
            s2.at[c, f, way, t], q2.at[c, f, way, t], dev_first(f, 1 - 2 * way),
        )

    def far_second(c, f, way):
        return remote(
            e3.at[c, f, way], r3.at[c, f, way],
            s3.at[c, f, way], q3.at[c, f, way], dev_second(f, 1 - 2 * way),
        )

    def near_second(c, f, way):
        return remote(
            e4.at[c, f, way], r4.at[c, f, way],
            s4.at[c, f, way], q4.at[c, f, way], dev_second(f, 1 - 2 * way),
        )

    def arrived(d, act):
        both = 1 if d in (0, turns) else 2

        @pl.loop(0, 2 * both)
        def _(i):
            step = d if both == 1 else d * (1 - 2 * lax.rem(i, 2))
            act((i // both) * nz + lax.rem(z + step + nz, nz))

    def send_far(c, d):
        def act(s):
            for f in range(2):
                ahead, t = place(f, s)

                @pl.when(ahead == 2)
                def _():
                    for way in range(2):
                        encode(e1.at[c, f, way, t], quarter_of(c, s, f, way)[...])
                        far(c, f, way, t).start()

        arrived(d, act)

    def send_near(c, k):
        for f in range(2):
            t = lax.rem(second(f) + OFFSETS[k], SIDE)
            for way in range(2):
                a = lax.rem(first(f) + 1 + 2 * way, SIDE)
                s = t * SIDE + a if f == 0 else a * SIDE + t
                encode(e2.at[c, f, way, t, 1 - way], quarter_of(c, s, f, 1 - way)[...])
                far(c, f, way, t).wait_recv()
                value = quarter_of(c, s, f, way)[...] + decode(r1.at[c, f, way, t])
                encode(e2.at[c, f, way, t, way], value)
                near(c, f, way, t).start()

    def turn(c, k):
        for f in range(2):
            t, s = own_block(f, k)
            for way in range(2):
                near(c, f, way, t).wait_recv()
            for q in range(2):
                own = quarter_of(c, s, f, q)
                own[...] = own[...] + (decode(r2.at[c, f, 0, t, q]) + decode(r2.at[c, f, 1, t, q]))
            if k == 0:
                for way in range(2):
                    encode(e3.at[c, f, way], quarter_of(c, s, f, way)[...])
                    far_second(c, f, way).start()
            elif k < 3:
                way = k - 1
                encode(e4.at[c, f, way, 1 - way], quarter_of(c, s, f, 1 - way)[...])
                far_second(c, f, way).wait_recv()
                value = quarter_of(c, s, f, way)[...] + decode(r3.at[c, f, way])
                encode(e4.at[c, f, way, way], value)
                near_second(c, f, way).start()

    def swap(c):
        return remote(mbuf.at[c, held], relay.at[c], ts.at[c, 0], tr.at[c, 0], taker)

    def swap_on(c):
        return remote(relay.at[c], match.at[c], ts.at[c, 1], tr.at[c, 1], onward)

    def send_match(c):
        @pl.when(moves)
        def _():
            swap(c).start()

        @pl.when(jnp.logical_not(moves))
        def _():
            relay[c] = mbuf[c, held]

    def pass_match(c):
        @pl.when(moves)
        def _():
            swap(c).wait_recv()

        @pl.when(goes_on)
        def _():
            swap_on(c).start()

        @pl.when(jnp.logical_not(goes_on))
        def _():
            match[c] = relay[c]

    def finish(c):
        for f in range(2):
            for way in range(2):
                near_second(c, f, way).wait_recv()
            for q in range(2):
                own = quarter_of(c, row, f, q)
                own[...] = own[...] + (decode(r4.at[c, f, 0, q]) + decode(r4.at[c, f, 1, q]))

    def write_covariance(c):
        product = pbuf.at[c, row]
        for i in range(blocks):
            keep = pattern[row, group * blocks + i].astype(jnp.float32)
            rows = pl.ds(i * block, block)
            cov[rows, pl.ds(c * LANES, LANES)] = -(product[rows, :] * keep)

    def diag_terms():
        @pl.when(goes_on)
        def _():
            for c in range(chunks):
                swap_on(c).wait_recv()

        columns = jnp.concatenate([match[c] for c in range(chunks)], axis=1)
        rest = jnp.concatenate([pbuf[c, row] for c in range(chunks)], axis=1)
        total = None
        for _ in range(3):
            top = rest.astype(jnp.bfloat16)
            rest = rest - top.astype(jnp.float32)
            add = lax.dot_general(
                columns, top, (((0,), (0,)), ((), ())), preferred_element_type=jnp.float32
            )
            total = add if total is None else total + add
        term[...] = total

    wide = block // 2

    def side(lf):
        return pl.ds(pl.multiple_of(lf * wide, wide), wide)

    def mine(owner):
        return pl.ds(pl.multiple_of(leaf * wide + owner * piece, piece), piece)

    def trade():
        return remote(term.at[side(1 - leaf), :], traded, ds.at[0], dr.at[0], other)

    def give(j):
        return remote(
            term.at[mine(lax.rem(z + j, nz)), :], dpart.at[j], ps.at[j], pr.at[j], z_dev(j)
        )

    def spread(j, owner):
        view = dsum.at[mine(owner), :]
        return remote(view, view, bs.at[j], br.at[j], z_dev(j))

    def hand(lf):
        view = dsum.at[side(lf), :]
        return remote(view, view, ds.at[1], dr.at[1], other)

    def diag_sum():
        trade().start()
        trade().wait_recv()
        term[side(leaf), :] = term[side(leaf), :] + traded[...]

        @pl.loop(1, nz)
        def _(j):
            give(j).start()

        for c in range(chunks):
            write_covariance(c)

        @pl.loop(1, nz)
        def _(j):
            give(j).wait_recv()

        dsum[mine(z), :] = dinv[0, mine(z), :] + (
            term[mine(z), :] + jnp.sum(dpart[pl.ds(1, nz - 1)], axis=0)
        )

        @pl.loop(1, nz)
        def _(j):
            spread(j, z).start()

        @pl.loop(1, nz)
        def _(j):
            spread(j, lax.rem(z - j + nz, nz)).wait_recv()

        hand(leaf).start()
        hand(1 - leaf).wait_recv()
        diag[0] = dsum[...]

    gather_begin(0)
    for d in range(turns):
        gather_step(0, d)
        if d == turns - 2:
            gather_begin(1)
        products(0, d)
        send_far(0, d)
    products(0, turns)
    send_far(0, turns)
    send_match(0)
    for d in range(turns):
        gather_step(1, d)
        send_near(0, d)
        products(1, d)
        send_far(1, d)
    products(1, turns)
    send_far(1, turns)
    send_match(1)
    pass_match(0)
    for k in range(SIDE):
        turn(0, k)
        send_near(1, k)
    finish(0)
    pass_match(1)
    for k in range(SIDE):
        turn(1, k)
    finish(1)
    diag_terms()
    diag_sum()

    for c in range(chunks):
        leaf_own(c, leaf).wait_send()
        for way in range(2):
            for j in range(pieces):
                z_copy(c, way, j, 0).wait_send()
                leaf_copy(c, way, j, leaf).wait_send()
            for f in range(2):
                for k in range(4):
                    far(c, f, way, k).wait_send()
                    near(c, f, way, k).wait_send()
                far_second(c, f, way).wait_send()
                near_second(c, f, way).wait_send()

        @pl.when(moves)
        def _():
            swap(c).wait_send()

        @pl.when(goes_on)
        def _():
            swap_on(c).wait_send()

    trade().wait_send()
    hand(leaf).wait_send()

    @pl.loop(1, nz)
    def _(j):
        give(j).wait_send()
        spread(j, z).wait_send()


def local(ancestor_inverse, panels, pattern, diag_inverse):
    depth, width = panels.shape
    rows_out = ancestor_inverse.shape[0]
    block = diag_inverse.shape[1]
    nz = lax.axis_size("col")
    groups = 2 * nz
    supers = pattern.shape[1]
    turned = pattern.T
    chunks = block // LANES
    half, quarter = depth // 2, depth // 4
    f32, bf16 = jnp.float32, jnp.bfloat16
    pieces = 2 * (nz // 2) - 1
    dma = pltpu.SemaphoreType.DMA
    vmem = pl.BlockSpec(memory_space=pltpu.VMEM)
    sums = [
        (chunks, 2, 2, 4, quarter + 16, LANES), (chunks, 2, 2, 4, 2, quarter + 16, LANES),
        (chunks, 2, 2, quarter + 16, LANES), (chunks, 2, 2, 2, quarter + 16, LANES),
    ]
    sems = [
        (chunks, 2, pieces), (chunks, 2 * pieces + 1),
        (chunks, 2, 2, 4), (chunks, 2, 2, 4), (chunks, 2, 2), (chunks, 2, 2),
        (chunks, 2), (2,), (nz,), (nz,),
    ]
    return tuple(pl.pallas_call(
        kernel,
        out_shape=(
            jax.ShapeDtypeStruct((rows_out, width), f32),
            jax.ShapeDtypeStruct(diag_inverse.shape, f32),
        ),
        in_specs=[pl.BlockSpec(memory_space=pltpu.SMEM), vmem, vmem, vmem],
        out_specs=(vmem, vmem),
        scratch_shapes=[
            pltpu.VMEM((chunks, supers, depth, LANES), bf16),
            pltpu.VMEM((chunks, depth, LANES), bf16),
            pltpu.VMEM((chunks, depth, LANES), bf16),
            pltpu.VMEM((chunks, supers, rows_out, LANES), f32),
        ] + [pltpu.VMEM(s, jnp.int16) for s in sums for _ in range(2)] + [
            pltpu.VMEM((block, block), f32),
            pltpu.VMEM((block // 2, block), f32),
            pltpu.VMEM((nz, block // groups, block), f32),
            pltpu.VMEM((block, block), f32),
        ] + [dma(s) for s in sems for _ in range(2)],
        compiler_params=pltpu.CompilerParams(
            collective_id=0, has_side_effects=True, vmem_limit_bytes=58 * 2**20
        ),
        cost_estimate=pl.CostEstimate(
            flops=2 * rows_out * depth * supers * block, bytes_accessed=8 * 2**20, transcendentals=0
        ),
    )(turned, ancestor_inverse, panels, diag_inverse))


def solution(mesh):
    placed = (P(("leaf", "col"), "row"), P("row", ("leaf", "col")), P(), P("row", None, None))
    return jax.shard_map(
        local,
        mesh=mesh,
        in_specs=placed,
        out_specs=(P(("leaf", "col"), "row"), P("row", None, None)),
        check_vma=False,
    )
```
